1024 devices in a mesh: wide: 64 (over z, core), narrow: 16 (over y, x).
Axes of the slice: x: 4, y: 4, z: 32, core: 2. Of those that a mesh axis runs over, the one named last changes fastest.
Arguments:
- audio: bfloat16 [131072, 1024], P(('wide', 'narrow')), may hold values from -0.25 to 0.25
- text: bfloat16 [131072, 1024], P(('wide', 'narrow')), may hold values from -0.25 to 0.25
- labels: int32 [131072], P(('wide', 'narrow')), may hold values from 0 to 32767
- route: int32 [131072, 1], P(('wide', 'narrow')), may hold values from 0 to 63; in each aligned block of 128 rows (0 to 127, 128 to 255, ...) at most 4 rows name the same one
- scale: float32 [1], replicated, may hold values from 8 to 16
- bias: float32 [1], replicated, may hold values from -2 to 0
Outputs:
- row_loss: float32 [131072], P(('wide', 'narrow'))
- audio_grad: float32 [131072, 1024], P(('wide', 'narrow'))
- text_grad: float32 [131072, 1024], P(('wide', 'narrow'))
The draws below stay inside these ranges and needn't reach their ends.
Inputs may be any that keep to these rules, and one draw needn't show every extreme that they name: route[j, 0] is a wide index; the holder has the narrow index of j's device. No device names one wide index with more than 4 of its rows, and some device names some wide index with exactly 4.
All inputs are finite; a program needn't handle non-finite values.
Results may differ from the reference program's by a relative error of at most 0.0045.
Values may be sent and summed in bfloat16 or wider, within the bound.
A program may use at most 64 MiB of HBM per device.

```python
import math
import jax
import jax.numpy as jnp
import numpy as np
from jax import lax

D = 1024
ROWS_DEV = 128
ROWS = 131072
MOST = 4
N_WIDE = 64
N_NARROW = 16
DEVICES = 1024


def set_ends(array, rng, smallest, largest):
    spot = [jax.random.randint(jax.random.fold_in(rng, axis), (), 0, length) for axis, length in enumerate(array.shape)]
    main_axis = array.shape.index(max(array.shape))
    next_to = spot[:main_axis] + [(spot[main_axis] + 1) % array.shape[main_axis]] + spot[main_axis + 1:]
    return array.at[tuple(spot)].set(smallest).at[tuple(next_to)].set(largest)


def steps_of(own_key, dims, cuts, low, high):
    level = 1.0
    for dim, shards_of in cuts:
        draws = jax.random.uniform(jax.random.fold_in(jax.random.fold_in(own_key, 6), dim), (shards_of,), jnp.float32, low / len(cuts), high / len(cuts))
        level = level * jnp.repeat(jnp.exp(draws), dims[dim] // shards_of).reshape((-1,) + (1,) * (len(dims) - 1 - dim))
    return level


def routed_block(key, own, number, rows, number_of, top, bound, lean):
    ranking = jax.random.permutation(key, number_of)
    heavy_load, common = portions_of(number_of, rows * top, bound, lean, True), portions_of(number_of, rows * top, bound, lean, False)
    places = jnp.arange(number_of)

    def named(sizes, rotation):
        used = int((sizes > 0).sum())
        fixed = max(1, used // 4)
        shifted = fixed + (places - fixed + rotation * (used - fixed)) % max(1, number_of - fixed)
        return jnp.zeros((number_of,), jnp.int32).at[ranking[jnp.where(places < fixed, places, shifted)]].set(jnp.asarray(sizes, jnp.int32))

    sizes = jnp.where(number % 4 == 0, named(heavy_load, number // 4), named(common, number - number // 4 - 1))
    mixed = jax.random.permutation(jax.random.fold_in(own, 3), number_of)
    source_of, sink = mixed[0:number_of // 2 * 2:2], mixed[1:number_of // 2 * 2:2]
    margin = jnp.minimum(sizes[source_of] - 1, bound - sizes[sink]) // 2
    margin = jnp.where((source_of == ranking[0]) | (sink == ranking[0]) | (sizes[sink] == 0), 0, jnp.maximum(margin, 0))
    shifted = jax.random.randint(jax.random.fold_in(own, 4), (number_of // 2,), 0, 1 << 20) % (margin + 1)
    sizes = sizes.at[source_of].add(-shifted).at[sink].add(shifted)
    items = jnp.searchsorted(jnp.cumsum(sizes), jnp.arange(rows * top), side="right").astype(jnp.int32)
    grid = items.reshape(top, rows).T
    grid = grid[jax.random.permutation(jax.random.fold_in(own, 1), rows)]
    rotation = jax.random.randint(jax.random.fold_in(own, 2), (rows, 1), 0, top)
    return jnp.take_along_axis(grid, (jnp.arange(top)[None, :] + rotation) % top, axis=1)


def portions_of(amount, total, bound, lean, full):
    loads = [(1 << 20) // math.isqrt(grade ** lean) + 1 for grade in range(1, amount + 1)]
    largest = bound if full else min(bound, max(-(-total // amount), total * loads[0] // sum(loads)))
    least = 1 if total - largest >= amount - 1 else 0
    given, spare = [largest] + [least] * (amount - 1), total - largest - least * (amount - 1)
    while spare > 0:
        free = [i for i in range(1, amount) if given[i] < largest] or [i for i in range(1, amount) if given[i] < bound]
        pool, budget = sum([loads[i] for i in free]), spare
        for i in free:
            more = min(bound - given[i], max(1, budget * loads[i] // pool), spare)
            given[i] = given[i] + more
            spare = spare - more
    return np.array(given)


def gaussian(key, shape, width, most, split=(), kind=jnp.bfloat16):
    array = jax.random.normal(key, shape, jnp.float32) * width
    if len(split) > 0:
        array = steps_of(key, shape, split, -0.22, 0.18) * array
    return jnp.clip(array, min=-most, max=most).astype(kind)


def setup_inputs(seed: int = 0) -> dict:
    keys = jax.random.split(jax.random.key(seed), 7)
    audio = gaussian(keys[0], (ROWS, D), 0.03125, 0.25, ((0, 1024),))
    text = gaussian(keys[1], (ROWS, D), 0.03125, 0.25, ((0, 1024),))
    labels = set_ends(jax.random.randint(keys[2], (ROWS,), 0, ROWS // 4), jax.random.fold_in(keys[2], 1), 0, (ROWS // 4) - 1).astype(jnp.int32)
    route_keys = jax.random.split(jax.random.fold_in(keys[3], 1), ROWS // ROWS_DEV)
    route_turns = jax.random.permutation(jax.random.fold_in(keys[3], 3), ROWS // ROWS_DEV)
    route = jax.vmap(lambda own, number: routed_block(jax.random.fold_in(keys[3], 2), own, number, ROWS_DEV, N_WIDE, 1, MOST, 2))(route_keys, route_turns).reshape((ROWS, 1))
    scale = jnp.clip(jax.random.uniform(keys[4], (1,), jnp.float32, 8.0, 16.0), 8.0, 16.0)
    bias = jnp.clip(jax.random.uniform(keys[5], (1,), jnp.float32, -2.0, 0.0), -2.0, 0.0)
    return {"audio": audio, "text": text, "labels": labels, "route": route, "scale": scale, "bias": bias}


EPSILON = 1e-06

def unit_rows(raw):
    values = raw.astype(jnp.float32)
    length = jnp.sqrt(lax.optimization_barrier(jnp.sum(values * values, axis=-1, keepdims=True)) + EPSILON)
    return (values / length, length)

def back_through_norm(unit, length, grad):
    return (grad - unit * lax.optimization_barrier(jnp.sum(unit * grad, axis=-1, keepdims=True))) / length

def tile_terms(audio_hat, audio_labels, text_block, text_labels, scale_value, bias_value):
    logits = scale_value * jnp.dot(audio_hat, text_block.T, preferred_element_type=jnp.float32) + bias_value
    matched = audio_labels[:, None] == text_labels[None, :]
    present = (text_labels >= 0)[None, :]
    signed = jnp.where(matched, 1.0, -1.0).astype(jnp.float32)
    losses = jnp.where(present, jax.nn.softplus(-signed * logits), 0.0)
    slope = jnp.where(present, jax.nn.sigmoid(logits) - matched.astype(jnp.float32), 0.0)
    weights = (scale_value * slope).astype(jnp.bfloat16)
    grad_audio = jnp.dot(weights, text_block, preferred_element_type=jnp.float32)
    grad_text = jnp.dot(weights.T, audio_hat, preferred_element_type=jnp.float32)
    return (lax.optimization_barrier(jnp.sum(losses, axis=1)), grad_audio, grad_text)

def reference(audio, text, labels, route, scale, bias):
    capacity = max(2, 2 * ROWS_DEV // N_WIDE)
    slots = N_WIDE * capacity
    group = ROWS_DEV * N_NARROW
    total_rows = ROWS_DEV * DEVICES
    audio_unit, audio_len = unit_rows(audio)
    text_unit, text_len = unit_rows(text)
    audio_hat = audio_unit.astype(jnp.bfloat16)
    text_hat = text_unit.astype(jnp.bfloat16)
    scale_value = scale[0]
    bias_value = bias[0]

    def group_block(inputs):
        audio_block, text_block, label_block = inputs
        return tile_terms(audio_block, label_block, text_block, label_block, scale_value, bias_value)
    own_loss, own_audio, own_text = lax.map(group_block, (audio_hat.reshape(N_WIDE, group, D), text_hat.reshape(N_WIDE, group, D), labels.reshape(N_WIDE, group)))
    own_loss = own_loss.reshape(total_rows)
    own_audio = own_audio.reshape(total_rows, D)
    own_text = own_text.reshape(total_rows, D)
    target = route[:, 0].astype(jnp.int32)
    order = jnp.arange(ROWS_DEV, dtype=jnp.int32)

    def rank_block(block):
        earlier = (block[:, None] == block[None, :]) & (order[:, None] > order[None, :])
        return lax.optimization_barrier(jnp.sum(earlier.astype(jnp.int32), axis=1))
    slot_rank = lax.map(rank_block, target.reshape(DEVICES, ROWS_DEV)).reshape(-1)
    index_all = jnp.arange(total_rows, dtype=jnp.int32)
    source = index_all // ROWS_DEV
    source_wide = source // N_NARROW
    source_narrow = source % N_NARROW
    holder_index = target * N_NARROW + source_narrow
    position = holder_index * slots + source_wide * capacity + slot_rank
    table = jnp.full((DEVICES * slots,), -1, jnp.int32).at[position].set(index_all).reshape(DEVICES, slots)

    def holder(carry, inputs):
        audio_block, label_block, entries = inputs
        present = entries >= 0
        safe = jnp.where(present, entries, 0).astype(jnp.int32)
        routed_text = jnp.where(present[:, None], text_hat[safe], jnp.zeros((), jnp.bfloat16))
        routed_labels = jnp.where(present, labels[safe], -1).astype(jnp.int32)
        loss_sum, grad_audio, grad_text = tile_terms(audio_block, label_block, routed_text, routed_labels, scale_value, bias_value)
        rounded = lax.optimization_barrier(grad_text.astype(jnp.bfloat16)).astype(jnp.float32)
        target_rows = jnp.where(present, entries, total_rows).astype(jnp.int32)
        carry = carry.at[target_rows].add(rounded, mode='drop')
        return (carry, (loss_sum, grad_audio))
    start = jnp.zeros((total_rows, D), jnp.float32)
    inputs = (audio_hat.reshape(DEVICES, ROWS_DEV, D), labels.reshape(DEVICES, ROWS_DEV), table)
    remote, (routed_loss, routed_audio) = lax.scan(holder, start, inputs)
    row_loss = (own_loss + routed_loss.reshape(total_rows)) / group
    audio_hat_grad = own_audio + routed_audio.reshape(total_rows, D)
    text_hat_grad = own_text + remote
    audio_grad = back_through_norm(audio_unit, audio_len, audio_hat_grad)
    text_grad = back_through_norm(text_unit, text_len, text_hat_grad)
    return (row_loss, audio_grad, text_grad)
```

```python
import functools
import math

import jax
import jax.numpy as jnp
from jax import lax
from jax.experimental import pallas as pl
from jax.experimental.pallas import tpu as pltpu
from jax.sharding import PartitionSpec as P

EPSILON = 1e-06
MESH = pl.DeviceIdType.MESH
LANES = 128
CAPACITY = 4
F32 = jnp.float32
BF16 = jnp.bfloat16


def unit_rows(raw):
    values = raw.astype(F32)
    length = jnp.sqrt(jnp.sum(values * values, axis=-1, keepdims=True) + EPSILON)
    return (values / length, length)


def back_through_norm(unit, length, grad):
    return (grad - unit * jnp.sum(unit * grad, axis=-1, keepdims=True)) / length


def dot_nt(a, b):
    return lax.dot_general(a, b, (((1,), (1,)), ((), ())), preferred_element_type=F32)


def dot_nn(a, b):
    return lax.dot_general(a, b, (((1,), (0,)), ((), ())), preferred_element_type=F32)


def dot_tn(a, b):
    return lax.dot_general(a, b, (((0,), (0,)), ((), ())), preferred_element_type=F32)


def iota(shape, axis):
    return lax.broadcasted_iota(jnp.int32, shape, axis)


def to_column(row):
    size = row.shape[1]
    eye = iota((size, size), 0) == iota((size, size), 1)
    return jnp.sum(jnp.where(eye, row, 0.0), axis=1, keepdims=True)


def to_row(column):
    size = column.shape[0]
    eye = iota((size, size), 0) == iota((size, size), 1)
    return jnp.sum(jnp.where(eye, column, 0.0), axis=0, keepdims=True)


def pair_terms(products, audio_labels, text_labels, scale, bias):
    logits = scale * products + bias
    matched = audio_labels == text_labels
    small = jnp.exp(-jnp.abs(logits))
    losses = jnp.maximum(jnp.where(matched, -logits, logits), 0.0) + jnp.log1p(small)
    sigmoid = jnp.where(logits >= 0.0, 1.0, small) / (1.0 + small)
    slope = sigmoid - jnp.where(matched, 1.0, 0.0)
    return (losses, slope)


def write_blocks(slab, out_ref, chunks):
    for half in range(chunks // 4):
        even, odd = [], []
        for g in (2 * half, 2 * half + 1):
            first, second = slab(2 * g), slab(2 * g + 1)
            first = first.reshape(-1, 8, LANES)
            second = second.reshape(-1, 8, LANES)
            low = iota(first.shape, 1) < CAPACITY
            even.append(jnp.where(low, first, pltpu.roll(second, CAPACITY, 1)))
            odd.append(jnp.where(low, pltpu.roll(first, CAPACITY, 1), second))
        rows = pl.ds(16 * half, 16)
        out_ref[:, 0, rows, :] = jnp.concatenate(even, axis=1).astype(BF16)
        out_ref[:, 1, rows, :] = jnp.concatenate(odd, axis=1).astype(BF16)


def read_blocks(in_ref, out_ref, chunks):
    for half in range(chunks // 4):
        rows = pl.ds(16 * half, 16)
        even = in_ref[:, 0, rows, :].astype(F32)
        odd = in_ref[:, 1, rows, :].astype(F32)
        for step in range(2):
            g = 2 * half + step
            e = even[:, 8 * step : 8 * step + 8, :]
            o = odd[:, 8 * step : 8 * step + 8, :]
            low = iota(e.shape, 1) < CAPACITY
            first = jnp.where(low, e, pltpu.roll(o, CAPACITY, 1))
            second = jnp.where(low, pltpu.roll(e, CAPACITY, 1), o)
            out_ref[:, pl.ds(2 * g * LANES, LANES)] = first.reshape(-1, LANES).astype(BF16)
            out_ref[:, pl.ds((2 * g + 1) * LANES, LANES)] = second.reshape(-1, LANES).astype(BF16)


def kernel(
    wide_size, side,
    scale_ref, bias_ref, audio_ref, text_ref, labels_ref, route_ref,
    loss_ref, audio_grad_ref, text_grad_ref,
    out_rows, in_rows, out_reply, in_reply, out_labels, in_labels, slots,
    audio_all, text_all, audio_labels, text_labels,
    weights, audio_sum, text_sum, loss_sum,
    audio_out, audio_in, text_out, text_in, loss_out, loss_in,
    rows_send, rows_recv, labels_send, labels_recv, reply_send, reply_recv,
    near_send, near_recv, local_sem,
):
    row_count, width = audio_ref.shape
    chunks = width // LANES
    group = row_count * side * side
    slot_count = wide_size * CAPACITY
    w = lax.axis_index("wide")
    n = lax.axis_index("narrow")
    y, x = n // side, n % side
    scale, bias = scale_ref[0], bias_ref[0]

    def far(k):
        return lax.rem(w + k, wide_size)

    def along_x(d):
        return lax.rem(x + d, side)

    def along_y(d):
        return lax.rem(y + d, side)

    barrier = pltpu.get_barrier_semaphore()

    def greet(k, carry):
        pl.semaphore_signal(barrier, inc=1, device_id=(far(k), n), device_id_type=MESH)
        return carry

    lax.fori_loop(1, wide_size, greet, 0)
    for d in range(1, side):
        pl.semaphore_signal(barrier, inc=1, device_id=(w, y * side + along_x(d)), device_id_type=MESH)
        pl.semaphore_signal(barrier, inc=1, device_id=(w, along_y(d) * side + x), device_id_type=MESH)

    text_hat = unit_rows(text_ref[...])[0].astype(BF16)
    text_all[y] = text_hat
    label_row = labels_ref[...].astype(F32)
    text_labels[y] = label_row
    audio_labels[x] = label_row
    target = route_ref[...].astype(F32)
    target_row = to_row(target)
    square = (row_count, row_count)
    same = target == target_row
    before = iota(square, 0) < iota(square, 1)
    after = iota(square, 0) > iota(square, 1)
    rank_row = jnp.sum(jnp.where(same & before, 1.0, 0.0), axis=0, keepdims=True)
    rank = jnp.sum(jnp.where(same & after, 1.0, 0.0), axis=1, keepdims=True)
    place_row = (target_row * CAPACITY + rank_row).astype(jnp.int32)
    place = (target * CAPACITY + rank).astype(jnp.int32)
    pick = jnp.where(iota((slot_count, row_count), 0) == place_row, 1.0, 0.0).astype(BF16)
    write_blocks(lambda c: dot_nn(pick, text_hat[:, c * LANES : (c + 1) * LANES]), out_rows, chunks)
    holder = iota((wide_size, row_count), 0) * CAPACITY
    lane = iota((wide_size, LANES), 1)
    packed = jnp.full((wide_size, LANES), -1.0, F32)
    for k in range(CAPACITY):
        found = jnp.where(holder + k == place_row, label_row + 1.0, 0.0)
        packed = jnp.where(lane == k, jnp.sum(found, axis=1, keepdims=True) - 1.0, packed)
    out_labels[...] = packed.reshape(wide_size, 1, LANES)

    pl.semaphore_wait(barrier, wide_size - 1 + 2 * (side - 1))

    def block_copy(src, dst, send, recv, k):
        peer = far(k)
        return pltpu.make_async_remote_copy(
            src_ref=src.at[peer // 2, peer % 2],
            dst_ref=dst.at[w // 2, w % 2],
            send_sem=send.at[k],
            recv_sem=recv.at[k],
            device_id=(peer, n),
            device_id_type=MESH,
        )

    def label_copy(k):
        peer = far(k)
        return pltpu.make_async_remote_copy(
            src_ref=out_labels.at[peer],
            dst_ref=in_labels.at[w],
            send_sem=labels_send.at[k],
            recv_sem=labels_recv.at[k],
            device_id=(peer, n),
            device_id_type=MESH,
        )

    def each(start, make, act):
        def step(k, carry):
            act(make(k))
            return carry

        lax.fori_loop(start, wide_size, step, 0)

    def rows_copy(k):
        return block_copy(out_rows, in_rows, rows_send, rows_recv, k)

    def reply_copy(k):
        return block_copy(out_reply, in_reply, reply_send, reply_recv, k)

    def start(copy):
        copy.start()

    def arrived(copy):
        copy.wait_recv()

    def left(copy):
        copy.wait_send()

    each(1, rows_copy, start)
    each(1, label_copy, start)
    own_rows = pltpu.make_async_copy(out_rows.at[w // 2, w % 2], in_rows.at[w // 2, w % 2], local_sem.at[0])
    own_rows.start()
    own_labels = pltpu.make_async_copy(out_labels.at[w], in_labels.at[w], local_sem.at[1])
    own_labels.start()

    def near_copy(kind, src, dst, d, on_x):
        peer = y * side + along_x(d) if on_x else along_y(d) * side + x
        return pltpu.make_async_remote_copy(
            src_ref=src,
            dst_ref=dst,
            send_sem=near_send.at[kind, d],
            recv_sem=near_recv.at[kind, d],
            device_id=(w, peer),
            device_id_type=MESH,
        )

    near = []
    for d in range(1, side):
        near.append(near_copy(0, text_all.at[y], text_all.at[y], d, False))
        near.append(near_copy(1, text_labels.at[y], text_labels.at[y], d, False))
        near.append(near_copy(2, audio_labels.at[x], audio_labels.at[x], d, True))
    for copy in near:
        copy.start()
    audio_hat = unit_rows(audio_ref[...])[0].astype(BF16)
    audio_all[x] = audio_hat
    shared = [near_copy(3, audio_all.at[x], audio_all.at[x], d, True) for d in range(1, side)]
    for copy in shared:
        copy.start()
    near += shared
    for copy in near:
        copy.wait_recv()

    block_rows = side * row_count
    text_block = text_all[...].reshape(block_rows, width)
    column_labels = jnp.concatenate([text_labels[t] for t in range(side)], axis=1)
    sent = []
    for d in range(side):
        owner = along_x(d)
        rows = audio_all[owner]
        losses, slope = pair_terms(
            dot_nt(rows, text_block), to_column(audio_labels[owner]), column_labels, scale, bias
        )
        block = (scale * slope).astype(BF16)
        for t in range(side):
            weights[t, owner] = block[:, t * row_count : (t + 1) * row_count]
        grad = dot_nn(block, text_block)
        loss = to_row(jnp.sum(losses, axis=1, keepdims=True))
        if d == 0:
            audio_sum[...] = grad
            loss_sum[...] = loss
        else:
            audio_out[d - 1] = grad.astype(BF16)
            loss_out[d - 1] = loss
            sent.append(near_copy(4, audio_out.at[d - 1], audio_in.at[d - 1], d, True))
            sent.append(near_copy(5, loss_out.at[d - 1], loss_in.at[d - 1], d, True))
            sent[-2].start()
            sent[-1].start()
    audio_block = audio_all[...].reshape(block_rows, width)
    for d in range(side):
        grad = dot_tn(weights[along_y(d)].reshape(block_rows, row_count), audio_block)
        if d == 0:
            text_sum[...] = grad
        else:
            text_out[d - 1] = grad.astype(BF16)
            sent.append(near_copy(6, text_out.at[d - 1], text_in.at[d - 1], d, False))
            sent[-1].start()

    own_labels.wait()
    own_rows.wait()
    each(1, label_copy, arrived)
    each(1, rows_copy, arrived)
    read_blocks(in_rows, slots, chunks)
    received = in_labels[...].reshape(wide_size, LANES)
    holder_slot = iota((wide_size, slot_count), 0) * CAPACITY
    slot_lane = iota((wide_size, slot_count), 1)
    slot_labels = jnp.zeros((1, slot_count), F32)
    for k in range(CAPACITY):
        found = jnp.where(slot_lane == holder_slot + k, received[:, k : k + 1], 0.0)
        slot_labels += jnp.sum(found, axis=0, keepdims=True)
    own_audio = audio_all[x]
    held = slots[...]
    losses, slope = pair_terms(
        dot_nt(own_audio, held), to_column(audio_labels[x]), slot_labels, scale, bias
    )
    present = slot_labels >= 0.0
    routed = (scale * jnp.where(present, slope, 0.0)).astype(BF16)
    write_blocks(
        lambda c: dot_tn(routed, audio_all[x, :, pl.ds(c * LANES, LANES)]), out_reply, chunks
    )
    each(1, reply_copy, start)
    own_reply = pltpu.make_async_copy(out_reply.at[w // 2, w % 2], in_reply.at[w // 2, w % 2], local_sem.at[0])
    own_reply.start()

    loss_sum[...] += to_row(jnp.sum(jnp.where(present, losses, 0.0), axis=1, keepdims=True))
    audio_sum[...] += dot_nn(routed, held)
    for copy in sent:
        copy.wait_recv()
    total = audio_sum[...]
    loss = loss_sum[...]
    for d in range(side - 1):
        total += audio_in[d].astype(F32)
        loss += loss_in[d]
    loss_ref[...] = loss / group
    audio_unit, audio_len = unit_rows(audio_ref[...])
    audio_grad_ref[...] = back_through_norm(audio_unit, audio_len, total)
    for d in range(side - 1):
        text_sum[...] += text_in[d].astype(F32)
    for copy in near + sent:
        copy.wait_send()
    each(1, rows_copy, left)
    each(1, label_copy, left)

    own_reply.wait()
    each(1, reply_copy, arrived)
    read_blocks(in_reply, slots, chunks)
    pick_back = jnp.where(iota((row_count, slot_count), 1) == place, 1.0, 0.0).astype(BF16)
    total = text_sum[...] + dot_nn(pick_back, slots[...])
    text_unit, text_len = unit_rows(text_ref[...])
    text_grad_ref[...] = back_through_norm(text_unit, text_len, total)
    each(1, reply_copy, left)


def body(audio, text, labels, route, scale, bias):
    row_count, width = audio.shape
    wide_size = lax.axis_size("wide")
    side = math.isqrt(lax.axis_size("narrow"))
    slot_count = wide_size * CAPACITY
    vmem = pl.BlockSpec(memory_space=pltpu.VMEM)
    smem = pl.BlockSpec(memory_space=pltpu.SMEM)
    blocks = pltpu.VMEM((wide_size // 2, 2, CAPACITY * width // LANES, LANES), BF16)
    wide_labels = pltpu.VMEM((wide_size, 1, LANES), F32)
    gathered = pltpu.VMEM((side, row_count, width), BF16)
    gathered_labels = pltpu.VMEM((side, 1, row_count), F32)
    term = pltpu.VMEM((row_count, width), F32)
    parts = pltpu.VMEM((side - 1, row_count, width), BF16)
    part_losses = pltpu.VMEM((side - 1, 1, row_count), F32)
    far_sem = pltpu.SemaphoreType.DMA((wide_size,))
    near_sem = pltpu.SemaphoreType.DMA((7, side))
    row_loss, audio_grad, text_grad = pl.pallas_call(
        functools.partial(kernel, wide_size, side),
        out_shape=(
            jax.ShapeDtypeStruct((1, row_count), F32),
            jax.ShapeDtypeStruct((row_count, width), F32),
            jax.ShapeDtypeStruct((row_count, width), F32),
        ),
        in_specs=[smem, smem, vmem, vmem, vmem, vmem],
        out_specs=(vmem, vmem, vmem),
        scratch_shapes=[
            blocks, blocks, blocks, blocks, wide_labels, wide_labels,
            pltpu.VMEM((slot_count, width), BF16),
            gathered, gathered, gathered_labels, gathered_labels,
            pltpu.VMEM((side, side, row_count, row_count), BF16),
            term, term, pltpu.VMEM((1, row_count), F32),
            parts, parts, parts, parts, part_losses, part_losses,
            far_sem, far_sem, far_sem, far_sem, far_sem, far_sem,
            near_sem, near_sem, pltpu.SemaphoreType.DMA((2,)),
        ],
        compiler_params=pltpu.CompilerParams(
            collective_id=0, has_side_effects=True, vmem_limit_bytes=48 * 2**20
        ),
    )(scale, bias, audio, text, labels.reshape(1, row_count), route)
    return (row_loss.reshape(row_count), audio_grad, text_grad)


def solution(mesh):
    rows = P(("wide", "narrow"), None)
    return jax.shard_map(
        body,
        mesh=mesh,
        in_specs=(rows, rows, P(("wide", "narrow")), rows, P(), P()),
        out_specs=(P(("wide", "narrow")), rows, rows),
        check_vma=False,
    )
```

```python
import functools
import math

import jax
import jax.numpy as jnp
from jax import lax
from jax.experimental import pallas as pl
from jax.experimental.pallas import tpu as pltpu
from jax.sharding import PartitionSpec as P

EPSILON = 1e-06
MESH = pl.DeviceIdType.MESH
LANES = 128
CAPACITY = 4
CHUNKS = 4
F32 = jnp.float32
BF16 = jnp.bfloat16


def unit_rows(raw):
    values = raw.astype(F32)
    length = jnp.sqrt(jnp.sum(values * values, axis=-1, keepdims=True) + EPSILON)
    return (values / length, length)


def back_through_norm(unit, length, grad):
    return (grad - unit * jnp.sum(unit * grad, axis=-1, keepdims=True)) / length


def dot_nt(a, b):
    return lax.dot_general(a, b, (((1,), (1,)), ((), ())), preferred_element_type=F32)


def dot_nn(a, b):
    return lax.dot_general(a, b, (((1,), (0,)), ((), ())), preferred_element_type=F32)


def dot_tn(a, b):
    return lax.dot_general(a, b, (((0,), (0,)), ((), ())), preferred_element_type=F32)


def iota(shape, axis):
    return lax.broadcasted_iota(jnp.int32, shape, axis)


def to_column(row):
    size = row.shape[1]
    eye = iota((size, size), 0) == iota((size, size), 1)
    return jnp.sum(jnp.where(eye, row, 0.0), axis=1, keepdims=True)


def to_row(column):
    size = column.shape[0]
    eye = iota((size, size), 0) == iota((size, size), 1)
    return jnp.sum(jnp.where(eye, column, 0.0), axis=0, keepdims=True)


def pair_terms(products, audio_labels, text_labels, scale, bias):
    logits = scale * products + bias
    matched = audio_labels == text_labels
    small = jnp.exp(-jnp.abs(logits))
    losses = jnp.maximum(jnp.where(matched, -logits, logits), 0.0) + jnp.log1p(small)
    sigmoid = jnp.where(logits >= 0.0, 1.0, small) / (1.0 + small)
    slope = sigmoid - jnp.where(matched, 1.0, 0.0)
    return (losses, slope)


def write_blocks(slab, out_ref, chunks, blocks):
    for half in range(chunks // 4):
        even, odd = [], []
        for g in (2 * half, 2 * half + 1):
            first, second = slab(2 * g), slab(2 * g + 1)
            first = first.reshape(-1, 8, LANES)
            second = second.reshape(-1, 8, LANES)
            low = iota(first.shape, 1) < CAPACITY
            even.append(jnp.where(low, first, pltpu.roll(second, CAPACITY, 1)))
            odd.append(jnp.where(low, pltpu.roll(first, CAPACITY, 1), second))
        rows = pl.ds(16 * half, 16)
        out_ref[blocks, 0, rows, :] = jnp.concatenate(even, axis=1).astype(BF16)
        out_ref[blocks, 1, rows, :] = jnp.concatenate(odd, axis=1).astype(BF16)


def read_blocks(in_ref, out_ref, chunks, blocks):
    span = pl.ds(blocks.start * 2 * CAPACITY, blocks.size * 2 * CAPACITY)
    for half in range(chunks // 4):
        rows = pl.ds(16 * half, 16)
        even = in_ref[blocks, 0, rows, :].astype(F32)
        odd = in_ref[blocks, 1, rows, :].astype(F32)
        for step in range(2):
            g = 2 * half + step
            e = even[:, 8 * step : 8 * step + 8, :]
            o = odd[:, 8 * step : 8 * step + 8, :]
            low = iota(e.shape, 1) < CAPACITY
            first = jnp.where(low, e, pltpu.roll(o, CAPACITY, 1))
            second = jnp.where(low, pltpu.roll(e, CAPACITY, 1), o)
            out_ref[span, pl.ds(2 * g * LANES, LANES)] = first.reshape(-1, LANES).astype(BF16)
            out_ref[span, pl.ds((2 * g + 1) * LANES, LANES)] = second.reshape(-1, LANES).astype(BF16)


def kernel(
    wide_size, side,
    scale_ref, bias_ref, audio_hbm, text_hbm, labels_hbm, route_hbm,
    loss_ref, audio_grad_ref, text_grad_ref,
    audio_ref, text_ref, labels_ref, route_ref,
    out_rows, in_rows, out_reply, in_reply, spare, slots,
    out_near, in_near, out_far, in_far,
    audio_all, text_all, audio_labels, text_labels,
    weights, audio_sum, text_sum, loss_sum,
    audio_out, audio_in, text_out, text_in, loss_out, loss_in,
    rows_send, rows_recv, reply_send, reply_recv,
    labels_send, labels_recv, near_send, near_recv, local_sem,
):
    row_count, width = audio_ref.shape
    chunks = width // LANES
    group = row_count * side * side
    slot_count = wide_size * CAPACITY
    pairs = wide_size // 2 // CHUNKS
    w = lax.axis_index("wide")
    n = lax.axis_index("narrow")
    y, x = n // side, n % side
    scale, bias = scale_ref[0], bias_ref[0]

    loads = [
        pltpu.make_async_copy(src, dst, local_sem.at[i])
        for i, (src, dst) in enumerate(
            [(text_hbm, text_ref), (route_hbm, route_ref), (labels_hbm, labels_ref), (audio_hbm, audio_ref)]
        )
    ]
    for load in loads:
        load.start()

    def ahead(k):
        return lax.rem(w + k, wide_size)

    def along_x(d):
        return lax.rem(x + d, side)

    def along_y(d):
        return lax.rem(y + d, side)

    def offset(p):
        q = wide_size - 1 - p
        return jnp.where(lax.rem(q, 2) == 0, q // 2, wide_size - 1 - q // 2)

    barrier = pltpu.get_barrier_semaphore()

    def greet(k, carry):
        pl.semaphore_signal(barrier, inc=1, device_id=(ahead(k), n), device_id_type=MESH)
        return carry

    lax.fori_loop(1, wide_size, greet, 0)
    for d in range(1, side):
        pl.semaphore_signal(barrier, inc=1, device_id=(w, y * side + along_x(d)), device_id_type=MESH)
        pl.semaphore_signal(barrier, inc=1, device_id=(w, along_y(d) * side + x), device_id_type=MESH)

    loads[0].wait()
    text_hat = unit_rows(text_ref[...])[0].astype(BF16)
    text_all[y] = text_hat
    loads[1].wait()
    target_row = route_ref[...]
    target = to_column(target_row.astype(F32)).astype(jnp.int32)
    square = (row_count, row_count)
    same = target == target_row
    before = iota(square, 0) < iota(square, 1)
    after = iota(square, 0) > iota(square, 1)
    rank_row = jnp.sum(jnp.where(same & before, 1.0, 0.0), axis=0, keepdims=True).astype(jnp.int32)
    rank = jnp.sum(jnp.where(same & after, 1.0, 0.0), axis=1, keepdims=True).astype(jnp.int32)

    def place_of(holder, source):
        k = holder - source
        k = jnp.where(k < 0, k + wide_size, k)
        return wide_size - 1 - jnp.where(k < wide_size // 2, 2 * k, 2 * (wide_size - k) - 1)

    slot_row = place_of(target_row, w) * CAPACITY + rank_row
    slot_column = place_of(target, w) * CAPACITY + rank
    pick = jnp.where(iota((slot_count, row_count), 0) == slot_row, 1.0, 0.0).astype(BF16)
    every = pl.ds(0, wide_size // 2)
    write_blocks(lambda c: dot_nn(pick, text_hat[:, c * LANES : (c + 1) * LANES]), out_rows, chunks, every)

    inner = 8 if wide_size >= 64 else 2
    outer = wide_size // inner
    a, b = w // inner, w % inner
    loads[2].wait()
    label_row = labels_ref[...].astype(F32)
    text_labels[y] = label_row
    audio_labels[x] = label_row
    label_column = to_column(label_row)
    label_lane = (target // inner) * CAPACITY + rank
    spread = jnp.where(iota((row_count, LANES), 1) == label_lane, label_column + 1.0, 0.0)
    for e in range(inner):
        found = jnp.where(target % inner == e, spread, 0.0)
        out_near[e] = jnp.sum(found, axis=0, keepdims=True) - 1.0
    in_near[b] = out_near[b]

    pl.semaphore_wait(barrier, wide_size - 1 + 2 * (side - 1))

    def wide_copy(src, dst, send, recv, peer):
        return pltpu.make_async_remote_copy(
            src_ref=src, dst_ref=dst, send_sem=send, recv_sem=recv, device_id=(peer, n), device_id_type=MESH
        )

    label_steps = []
    for e in range(1, inner):
        f = lax.rem(b + e, inner)
        label_steps.append(
            wide_copy(out_near.at[f], in_near.at[b], labels_send.at[0, e], labels_recv.at[0, e], a * inner + f)
        )
    for copy in label_steps:
        copy.start()

    def start_blocks(src, dst, send, recv, chunk, sign):
        def step(p, carry):
            peer = lax.rem(w + wide_size + sign * offset(p), wide_size)
            wide_copy(src.at[p // 2, p % 2], dst.at[p // 2, p % 2], send.at[0], recv.at[chunk], peer).start()
            return carry

        first = chunk * 2 * pairs
        lax.fori_loop(first, min(first + 2 * pairs, wide_size - 1), step, 0)
        if chunk == CHUNKS - 1:
            pltpu.make_async_copy(src.at[wide_size // 2 - 1, 1], dst.at[wide_size // 2 - 1, 1], recv.at[CHUNKS - 1]).start()
            pltpu.make_async_copy(src.at[wide_size // 2 - 1, 1], spare.at[(1 - sign) // 2], send.at[0]).start()

    def wait_blocks(dst, recv, chunk):
        whole = dst.at[pl.ds(chunk * pairs, pairs)]
        pltpu.make_async_copy(whole, whole, recv.at[chunk]).wait()

    start_blocks(out_rows, in_rows, rows_send, rows_recv, 0, 1)

    def near_copy(kind, src, dst, d, on_x):
        peer = y * side + along_x(d) if on_x else along_y(d) * side + x
        return pltpu.make_async_remote_copy(
            src_ref=src,
            dst_ref=dst,
            send_sem=near_send.at[kind, d],
            recv_sem=near_recv.at[kind, d],
            device_id=(w, peer),
            device_id_type=MESH,
        )

    near = []
    for d in range(1, side):
        near.append(near_copy(0, text_all.at[y], text_all.at[y], d, False))
        near.append(near_copy(1, text_labels.at[y], text_labels.at[y], d, False))
        near.append(near_copy(2, audio_labels.at[x], audio_labels.at[x], d, True))
    for copy in near:
        copy.start()
    loads[3].wait()
    audio_hat = unit_rows(audio_ref[...])[0].astype(BF16)
    audio_all[x] = audio_hat
    shared = [near_copy(3, audio_all.at[x], audio_all.at[x], d, True) for d in range(1, side)]
    for copy in shared:
        copy.start()
    near += shared

    for copy in label_steps:
        copy.wait_recv()
    heard = in_near[...].reshape(inner, LANES)
    turned = {d: pltpu.roll(heard, (d * CAPACITY) % LANES, 1) for d in range(1 - outer, inner)}
    source = iota((inner, LANES), 0)
    mine = iota((inner, LANES), 1) // CAPACITY == source
    for h in range(outer):
        row = jnp.zeros((inner, LANES), F32)
        for e in range(inner):
            row = jnp.where(mine & (source == e), turned[e - h], row)
        out_far[h] = jnp.sum(row, axis=0, keepdims=True)
    in_far[a] = out_far[a]
    for d in range(1, outer):
        h = lax.rem(a + d, outer)
        label_steps.append(
            wide_copy(out_far.at[h], in_far.at[a], labels_send.at[1, d], labels_recv.at[1, d], h * inner + b)
        )
        label_steps[-1].start()
    for chunk in range(1, CHUNKS):
        start_blocks(out_rows, in_rows, rows_send, rows_recv, chunk, 1)

    for copy in near:
        copy.wait_recv()

    block_rows = side * row_count
    text_block = text_all[...].reshape(block_rows, width)
    column_labels = jnp.concatenate([text_labels[t] for t in range(side)], axis=1)
    sent = []
    for d in range(side):
        owner = along_x(d)
        rows = audio_all[owner]
        losses, slope = pair_terms(
            dot_nt(rows, text_block), to_column(audio_labels[owner]), column_labels, scale, bias
        )
        block = (scale * slope).astype(BF16)
        for t in range(side):
            weights[t, owner] = block[:, t * row_count : (t + 1) * row_count]
        grad = dot_nn(block, text_block)
        loss = to_row(jnp.sum(losses, axis=1, keepdims=True))
        if d == 0:
            audio_sum[...] = grad
            loss_sum[...] = loss
        else:
            audio_out[d - 1] = grad.astype(BF16)
            loss_out[d - 1] = loss
            sent.append(near_copy(4, audio_out.at[d - 1], audio_in.at[d - 1], d, True))
            sent.append(near_copy(5, loss_out.at[d - 1], loss_in.at[d - 1], d, True))
            sent[-2].start()
            sent[-1].start()
    audio_block = audio_all[...].reshape(block_rows, width)
    for d in range(side):
        grad = dot_tn(weights[along_y(d)].reshape(block_rows, row_count), audio_block)
        if d == 0:
            text_sum[...] = grad
        else:
            text_out[d - 1] = grad.astype(BF16)
            sent.append(near_copy(6, text_out.at[d - 1], text_in.at[d - 1], d, False))
            sent[-1].start()

    for copy in label_steps[inner - 1 :]:
        copy.wait_recv()
    share = inner * CAPACITY
    per_row = max(1, LANES // share)
    pieces = []
    for first in range(0, outer, per_row):
        row = jnp.zeros((1, LANES), F32)
        for h in range(first, min(first + per_row, outer)):
            moved = pltpu.roll(in_far[h], ((h - first) * share) % LANES, 1)
            row = jnp.where(iota((1, LANES), 1) // share == h - first, moved, row)
        pieces.append(row)
    by_source = jnp.concatenate(pieces, axis=1)[:, :slot_count]
    slot = iota((slot_count, slot_count), 0)
    here = place_of(w, slot // CAPACITY) * CAPACITY + slot % CAPACITY
    moved = jnp.where(here == iota((slot_count, slot_count), 1), to_column(by_source), 0.0)
    slot_labels = jnp.sum(moved, axis=0, keepdims=True)
    own_audio = audio_all[x]
    own_labels = to_column(audio_labels[x])
    for chunk in range(CHUNKS):
        span = slice(chunk * 2 * pairs * CAPACITY, (chunk + 1) * 2 * pairs * CAPACITY)
        blocks = pl.ds(chunk * pairs, pairs)
        labels = slot_labels[:, span]
        present = labels >= 0.0
        wait_blocks(in_rows, rows_recv, chunk)
        read_blocks(in_rows, slots, chunks, blocks)
        held = slots[span]
        losses, slope = pair_terms(dot_nt(own_audio, held), own_labels, labels, scale, bias)
        routed = (scale * jnp.where(present, slope, 0.0)).astype(BF16)
        write_blocks(
            lambda c: dot_tn(routed, audio_all[x, :, pl.ds(c * LANES, LANES)]), out_reply, chunks, blocks
        )
        start_blocks(out_reply, in_reply, reply_send, reply_recv, chunk, -1)
        loss_sum[...] += to_row(jnp.sum(jnp.where(present, losses, 0.0), axis=1, keepdims=True))
        audio_sum[...] += dot_nn(routed, held)

    for copy in sent:
        copy.wait_recv()
    total = audio_sum[...]
    loss = loss_sum[...]
    for d in range(side - 1):
        total += audio_in[d].astype(F32)
        loss += loss_in[d]
    loss_ref[...] = loss / group
    audio_unit, audio_len = unit_rows(audio_ref[...])
    audio_grad_ref[...] = back_through_norm(audio_unit, audio_len, total)
    for d in range(side - 1):
        text_sum[...] += text_in[d].astype(F32)
    for copy in near + sent + label_steps:
        copy.wait_send()
    pltpu.make_async_copy(out_rows, out_rows, rows_send.at[0]).wait()

    pick_back = jnp.where(iota((row_count, slot_count), 1) == slot_column, 1.0, 0.0).astype(BF16)
    total = text_sum[...]
    for chunk in range(CHUNKS):
        span = slice(chunk * 2 * pairs * CAPACITY, (chunk + 1) * 2 * pairs * CAPACITY)
        wait_blocks(in_reply, reply_recv, chunk)
        read_blocks(in_reply, slots, chunks, pl.ds(chunk * pairs, pairs))
        total += dot_nn(pick_back[:, span], slots[span])
    text_unit, text_len = unit_rows(text_ref[...])
    text_grad_ref[...] = back_through_norm(text_unit, text_len, total)
    pltpu.make_async_copy(out_reply, out_reply, reply_send.at[0]).wait()


def body(audio, text, labels, route, scale, bias):
    row_count, width = audio.shape
    wide_size = lax.axis_size("wide")
    side = math.isqrt(lax.axis_size("narrow"))
    slot_count = wide_size * CAPACITY
    vmem = pl.BlockSpec(memory_space=pltpu.VMEM)
    smem = pl.BlockSpec(memory_space=pltpu.SMEM)
    blocks = pltpu.VMEM((wide_size // 2, 2, CAPACITY * width // LANES, LANES), BF16)
    inner = 8 if wide_size >= 64 else 2
    near_labels = pltpu.VMEM((inner, 1, LANES), F32)
    far_labels = pltpu.VMEM((wide_size // inner, 1, LANES), F32)
    rows = pltpu.VMEM((row_count, width), BF16)
    numbers = pltpu.VMEM((1, row_count), jnp.int32)
    whole = pl.BlockSpec(memory_space=pl.ANY)
    gathered = pltpu.VMEM((side, row_count, width), BF16)
    gathered_labels = pltpu.VMEM((side, 1, row_count), F32)
    term = pltpu.VMEM((row_count, width), F32)
    parts = pltpu.VMEM((side - 1, row_count, width), BF16)
    part_losses = pltpu.VMEM((side - 1, 1, row_count), F32)
    one_sem = pltpu.SemaphoreType.DMA((1,))
    chunk_sem = pltpu.SemaphoreType.DMA((CHUNKS,))
    label_sem = pltpu.SemaphoreType.DMA((2, max(inner, wide_size // inner)))
    near_sem = pltpu.SemaphoreType.DMA((7, side))
    row_loss, audio_grad, text_grad = pl.pallas_call(
        functools.partial(kernel, wide_size, side),
        out_shape=(
            jax.ShapeDtypeStruct((1, row_count), F32),
            jax.ShapeDtypeStruct((row_count, width), F32),
            jax.ShapeDtypeStruct((row_count, width), F32),
        ),
        in_specs=[smem, smem, whole, whole, whole, whole],
        out_specs=(vmem, vmem, vmem),
        scratch_shapes=[
            rows, rows, numbers, numbers,
            blocks, blocks, blocks, blocks, pltpu.VMEM((2, CAPACITY * width // LANES, LANES), BF16),
            pltpu.VMEM((slot_count, width), BF16),
            near_labels, near_labels, far_labels, far_labels,
            gathered, gathered, gathered_labels, gathered_labels,
            pltpu.VMEM((side, side, row_count, row_count), BF16),
            term, term, pltpu.VMEM((1, row_count), F32),
            parts, parts, parts, parts, part_losses, part_losses,
            one_sem, chunk_sem, one_sem, chunk_sem,
            label_sem, label_sem, near_sem, near_sem, pltpu.SemaphoreType.DMA((4,)),
        ],
        compiler_params=pltpu.CompilerParams(
            collective_id=0, has_side_effects=True, vmem_limit_bytes=56 * 2**20
        ),
    )(scale, bias, audio, text, labels.reshape(1, row_count), route.reshape(1, row_count))
    return (row_loss.reshape(row_count), audio_grad, text_grad)


def solution(mesh):
    rows = P(("wide", "narrow"), None)
    return jax.shard_map(
        body,
        mesh=mesh,
        in_specs=(rows, rows, P(("wide", "narrow")), rows, P(), P()),
        out_specs=(P(("wide", "narrow")), rows, rows),
        check_vma=False,
    )
```

```python
import functools
import math

import jax
import jax.numpy as jnp
from jax import lax
from jax.experimental import pallas as pl
from jax.experimental.pallas import tpu as pltpu
from jax.sharding import PartitionSpec as P

EPSILON = 1e-06
MESH = pl.DeviceIdType.MESH
LANES = 128
CAPACITY = 4
CHUNKS = 4
EARLY = 8
F32 = jnp.float32
BF16 = jnp.bfloat16


def unit_rows(raw):
    values = raw.astype(F32)
    length = jnp.sqrt(jnp.sum(values * values, axis=-1, keepdims=True) + EPSILON)
    return (values / length, length)


def back_through_norm(unit, length, grad):
    return (grad - unit * jnp.sum(unit * grad, axis=-1, keepdims=True)) / length


def dot_nt(a, b):
    return lax.dot_general(a, b, (((1,), (1,)), ((), ())), preferred_element_type=F32)


def dot_nn(a, b):
    return lax.dot_general(a, b, (((1,), (0,)), ((), ())), preferred_element_type=F32)


def dot_tn(a, b):
    return lax.dot_general(a, b, (((0,), (0,)), ((), ())), preferred_element_type=F32)


def iota(shape, axis):
    return lax.broadcasted_iota(jnp.int32, shape, axis)


def to_column(row):
    size = row.shape[1]
    eye = iota((size, size), 0) == iota((size, size), 1)
    return jnp.sum(jnp.where(eye, row, 0.0), axis=1, keepdims=True)


def to_row(column):
    size = column.shape[0]
    eye = iota((size, size), 0) == iota((size, size), 1)
    return jnp.sum(jnp.where(eye, column, 0.0), axis=0, keepdims=True)


def pair_terms(products, audio_labels, text_labels, scale, bias):
    logits = scale * products + bias
    matched = audio_labels == text_labels
    small = jnp.exp(-jnp.abs(logits))
    losses = jnp.maximum(jnp.where(matched, -logits, logits), 0.0) + jnp.log1p(small)
    sigmoid = jnp.where(logits >= 0.0, 1.0, small) / (1.0 + small)
    slope = sigmoid - jnp.where(matched, 1.0, 0.0)
    return (losses, slope)


def write_blocks(slab, out_ref, chunks, blocks):
    for half in range(chunks // 4):
        even, odd = [], []
        for g in (2 * half, 2 * half + 1):
            first, second = slab(2 * g), slab(2 * g + 1)
            first = first.reshape(-1, 8, LANES)
            second = second.reshape(-1, 8, LANES)
            low = iota(first.shape, 1) < CAPACITY
            even.append(jnp.where(low, first, pltpu.roll(second, CAPACITY, 1)))
            odd.append(jnp.where(low, pltpu.roll(first, CAPACITY, 1), second))
        rows = pl.ds(16 * half, 16)
        out_ref[blocks, 0, rows, :] = jnp.concatenate(even, axis=1).astype(BF16)
        out_ref[blocks, 1, rows, :] = jnp.concatenate(odd, axis=1).astype(BF16)


def read_blocks(in_ref, out_ref, chunks, blocks):
    span = pl.ds(blocks.start * 2 * CAPACITY, blocks.size * 2 * CAPACITY)
    for half in range(chunks // 4):
        rows = pl.ds(16 * half, 16)
        even = in_ref[blocks, 0, rows, :].astype(F32)
        odd = in_ref[blocks, 1, rows, :].astype(F32)
        for step in range(2):
            g = 2 * half + step
            e = even[:, 8 * step : 8 * step + 8, :]
            o = odd[:, 8 * step : 8 * step + 8, :]
            low = iota(e.shape, 1) < CAPACITY
            first = jnp.where(low, e, pltpu.roll(o, CAPACITY, 1))
            second = jnp.where(low, pltpu.roll(e, CAPACITY, 1), o)
            out_ref[span, pl.ds(2 * g * LANES, LANES)] = first.reshape(-1, LANES).astype(BF16)
            out_ref[span, pl.ds((2 * g + 1) * LANES, LANES)] = second.reshape(-1, LANES).astype(BF16)


def kernel(
    wide_size, side,
    scale_ref, bias_ref, audio_hbm, text_hbm, labels_hbm, route_hbm,
    loss_ref, audio_grad_ref, text_grad_ref,
    audio_ref, text_ref, labels_ref, route_ref,
    out_rows, in_rows, out_reply, in_reply, spare, slots,
    out_near, in_near, out_far, in_far,
    audio_all, text_all, audio_labels, text_labels,
    weights, audio_sum, text_sum, loss_sum,
    audio_out, audio_in, text_out, text_in, loss_out, loss_in,
    rows_send, rows_recv, reply_send, reply_recv,
    labels_send, labels_recv, near_send, near_recv, local_sem,
):
    row_count, width = audio_ref.shape
    chunks = width // LANES
    group = row_count * side * side
    slot_count = wide_size * CAPACITY
    pairs = wide_size // 2 // CHUNKS
    w = lax.axis_index("wide")
    n = lax.axis_index("narrow")
    y, x = n // side, n % side
    scale, bias = scale_ref[0], bias_ref[0]

    loads = [
        pltpu.make_async_copy(src, dst, local_sem.at[i])
        for i, (src, dst) in enumerate(
            [(text_hbm, text_ref), (route_hbm, route_ref), (labels_hbm, labels_ref), (audio_hbm, audio_ref)]
        )
    ]
    for load in loads:
        load.start()

    def ahead(k):
        return lax.rem(w + k, wide_size)

    def along_x(d):
        return lax.rem(x + d, side)

    def along_y(d):
        return lax.rem(y + d, side)

    def offset(p):
        q = wide_size - 1 - p
        return jnp.where(lax.rem(q, 2) == 0, q // 2, wide_size - 1 - q // 2)

    barrier = pltpu.get_barrier_semaphore()

    def greet(k, carry):
        pl.semaphore_signal(barrier, inc=1, device_id=(ahead(k), n), device_id_type=MESH)
        return carry

    lax.fori_loop(1, wide_size, greet, 0)
    for d in range(1, side):
        pl.semaphore_signal(barrier, inc=1, device_id=(w, y * side + along_x(d)), device_id_type=MESH)
        pl.semaphore_signal(barrier, inc=1, device_id=(w, along_y(d) * side + x), device_id_type=MESH)

    loads[0].wait()
    text_hat = unit_rows(text_ref[...])[0].astype(BF16)
    text_all[y] = text_hat
    loads[1].wait()
    target_row = route_ref[...]
    target = to_column(target_row.astype(F32)).astype(jnp.int32)
    square = (row_count, row_count)
    same = target == target_row
    before = iota(square, 0) < iota(square, 1)
    after = iota(square, 0) > iota(square, 1)
    rank_row = jnp.sum(jnp.where(same & before, 1.0, 0.0), axis=0, keepdims=True).astype(jnp.int32)
    rank = jnp.sum(jnp.where(same & after, 1.0, 0.0), axis=1, keepdims=True).astype(jnp.int32)

    def place_of(holder, source):
        k = holder - source
        k = jnp.where(k < 0, k + wide_size, k)
        return wide_size - 1 - jnp.where(k < wide_size // 2, 2 * k, 2 * (wide_size - k) - 1)

    half, quarter = wide_size // 2, wide_size // 4

    def swapped(p, device, other, late):
        i = p - quarter
        back = late(i)
        p = jnp.where((i >= 0) & (i < EARLY) & (device >= EARLY) & (back >= half), back, p)
        return jnp.where((i >= quarter) & (other < EARLY) & (device >= EARLY), quarter + other, p)

    def sender_place(p, source, holder):
        return swapped(p, source, holder, lambda i: place_of(i, source))

    def holder_place(p, holder, source):
        return swapped(p, holder, source, lambda i: place_of(holder, i))

    slot_row = sender_place(place_of(target_row, w), w, target_row) * CAPACITY + rank_row
    slot_column = sender_place(place_of(target, w), w, target) * CAPACITY + rank
    pick = jnp.where(iota((slot_count, row_count), 0) == slot_row, 1.0, 0.0).astype(BF16)
    every = pl.ds(0, wide_size // 2)
    write_blocks(lambda c: dot_nn(pick, text_hat[:, c * LANES : (c + 1) * LANES]), out_rows, chunks, every)

    inner = 8 if wide_size >= 64 else 2
    outer = wide_size // inner
    a, b = w // inner, w % inner
    loads[2].wait()
    label_row = labels_ref[...].astype(F32)
    text_labels[y] = label_row
    audio_labels[x] = label_row
    label_column = to_column(label_row)
    label_lane = (target // inner) * CAPACITY + rank
    spread = jnp.where(iota((row_count, LANES), 1) == label_lane, label_column + 1.0, 0.0)
    for e in range(inner):
        found = jnp.where(target % inner == e, spread, 0.0)
        out_near[e] = jnp.sum(found, axis=0, keepdims=True) - 1.0
    in_near[b] = out_near[b]

    pl.semaphore_wait(barrier, wide_size - 1 + 2 * (side - 1))

    def wide_copy(src, dst, send, recv, peer):
        return pltpu.make_async_remote_copy(
            src_ref=src, dst_ref=dst, send_sem=send, recv_sem=recv, device_id=(peer, n), device_id_type=MESH
        )

    label_steps = []
    for e in range(1, inner):
        f = lax.rem(b + e, inner)
        label_steps.append(
            wide_copy(out_near.at[f], in_near.at[b], labels_send.at[0, e], labels_recv.at[0, e], a * inner + f)
        )
    for copy in label_steps:
        copy.start()

    def start_blocks(src, dst, send, recv, chunk, sign):
        def step(p, carry):
            if sign > 0:
                place = sender_place(p, w, ahead(offset(p)))
                peer = ahead(offset(place))
                there = holder_place(place, peer, w)
            else:
                place = holder_place(p, w, ahead(wide_size - offset(p)))
                peer = ahead(wide_size - offset(place))
                there = sender_place(place, peer, w)
            wide_copy(
                src.at[p // 2, p % 2], dst.at[there // 2, there % 2], send.at[0], recv.at[there // (2 * pairs)], peer
            ).start()
            return carry

        own = wide_size - 1
        first = chunk * 2 * pairs
        lax.fori_loop(first, min(first + 2 * pairs, own), step, 0)
        if chunk == CHUNKS - 1:
            block = src.at[own // 2, own % 2]
            pltpu.make_async_copy(block, dst.at[own // 2, own % 2], recv.at[chunk]).start()
            pltpu.make_async_copy(block, spare.at[(1 - sign) // 2], send.at[0]).start()

    def wait_blocks(dst, recv, chunk):
        whole = dst.at[pl.ds(chunk * pairs, pairs)]
        pltpu.make_async_copy(whole, whole, recv.at[chunk]).wait()

    start_blocks(out_rows, in_rows, rows_send, rows_recv, 0, 1)

    def near_copy(kind, src, dst, d, on_x):
        peer = y * side + along_x(d) if on_x else along_y(d) * side + x
        return pltpu.make_async_remote_copy(
            src_ref=src,
            dst_ref=dst,
            send_sem=near_send.at[kind, d],
            recv_sem=near_recv.at[kind, d],
            device_id=(w, peer),
            device_id_type=MESH,
        )

    near = []
    for d in range(1, side):
        near.append(near_copy(0, text_all.at[y], text_all.at[y], d, False))
        near.append(near_copy(1, text_labels.at[y], text_labels.at[y], d, False))
        near.append(near_copy(2, audio_labels.at[x], audio_labels.at[x], d, True))
    for copy in near:
        copy.start()
    loads[3].wait()
    audio_hat = unit_rows(audio_ref[...])[0].astype(BF16)
    audio_all[x] = audio_hat
    shared = [near_copy(3, audio_all.at[x], audio_all.at[x], d, True) for d in range(1, side)]
    for copy in shared:
        copy.start()
    near += shared

    for copy in label_steps:
        copy.wait_recv()
    heard = in_near[...].reshape(inner, LANES)
    turned = {d: pltpu.roll(heard, (d * CAPACITY) % LANES, 1) for d in range(1 - outer, inner)}
    source = iota((inner, LANES), 0)
    mine = iota((inner, LANES), 1) // CAPACITY == source
    for h in range(outer):
        row = jnp.zeros((inner, LANES), F32)
        for e in range(inner):
            row = jnp.where(mine & (source == e), turned[e - h], row)
        out_far[h] = jnp.sum(row, axis=0, keepdims=True)
    in_far[a] = out_far[a]
    for d in range(1, outer):
        h = lax.rem(a + d, outer)
        label_steps.append(
            wide_copy(out_far.at[h], in_far.at[a], labels_send.at[1, d], labels_recv.at[1, d], h * inner + b)
        )
        label_steps[-1].start()
    for chunk in range(1, CHUNKS):
        start_blocks(out_rows, in_rows, rows_send, rows_recv, chunk, 1)

    for copy in near:
        copy.wait_recv()

    block_rows = side * row_count
    text_block = text_all[...].reshape(block_rows, width)
    column_labels = jnp.concatenate([text_labels[t] for t in range(side)], axis=1)
    sent = []
    for d in range(side):
        owner = along_x(d)
        rows = audio_all[owner]
        losses, slope = pair_terms(
            dot_nt(rows, text_block), to_column(audio_labels[owner]), column_labels, scale, bias
        )
        block = (scale * slope).astype(BF16)
        for t in range(side):
            weights[t, owner] = block[:, t * row_count : (t + 1) * row_count]
        grad = dot_nn(block, text_block)
        loss = to_row(jnp.sum(losses, axis=1, keepdims=True))
        if d == 0:
            audio_sum[...] = grad
            loss_sum[...] = loss
        else:
            audio_out[d - 1] = grad.astype(BF16)
            loss_out[d - 1] = loss
            sent.append(near_copy(4, audio_out.at[d - 1], audio_in.at[d - 1], d, True))
            sent.append(near_copy(5, loss_out.at[d - 1], loss_in.at[d - 1], d, True))
            sent[-2].start()
            sent[-1].start()
    audio_block = audio_all[...].reshape(block_rows, width)
    for d in range(side):
        grad = dot_tn(weights[along_y(d)].reshape(block_rows, row_count), audio_block)
        if d == 0:
            text_sum[...] = grad
        else:
            text_out[d - 1] = grad.astype(BF16)
            sent.append(near_copy(6, text_out.at[d - 1], text_in.at[d - 1], d, False))
            sent[-1].start()

    for copy in label_steps[inner - 1 :]:
        copy.wait_recv()
    share = inner * CAPACITY
    per_row = max(1, LANES // share)
    pieces = []
    for first in range(0, outer, per_row):
        row = jnp.zeros((1, LANES), F32)
        for h in range(first, min(first + per_row, outer)):
            moved = pltpu.roll(in_far[h], ((h - first) * share) % LANES, 1)
            row = jnp.where(iota((1, LANES), 1) // share == h - first, moved, row)
        pieces.append(row)
    by_source = jnp.concatenate(pieces, axis=1)[:, :slot_count]
    slot = iota((slot_count, slot_count), 0)
    here = holder_place(place_of(w, slot // CAPACITY), w, slot // CAPACITY) * CAPACITY + slot % CAPACITY
    moved = jnp.where(here == iota((slot_count, slot_count), 1), to_column(by_source), 0.0)
    slot_labels = jnp.sum(moved, axis=0, keepdims=True)
    own_audio = audio_all[x]
    own_labels = to_column(audio_labels[x])
    for chunk in range(CHUNKS):
        span = slice(chunk * 2 * pairs * CAPACITY, (chunk + 1) * 2 * pairs * CAPACITY)
        blocks = pl.ds(chunk * pairs, pairs)
        labels = slot_labels[:, span]
        present = labels >= 0.0
        wait_blocks(in_rows, rows_recv, chunk)
        read_blocks(in_rows, slots, chunks, blocks)
        held = slots[span]
        losses, slope = pair_terms(dot_nt(own_audio, held), own_labels, labels, scale, bias)
        routed = (scale * jnp.where(present, slope, 0.0)).astype(BF16)
        write_blocks(
            lambda c: dot_tn(routed, audio_all[x, :, pl.ds(c * LANES, LANES)]), out_reply, chunks, blocks
        )
        start_blocks(out_reply, in_reply, reply_send, reply_recv, chunk, -1)
        loss_sum[...] += to_row(jnp.sum(jnp.where(present, losses, 0.0), axis=1, keepdims=True))
        audio_sum[...] += dot_nn(routed, held)

    for copy in sent:
        copy.wait_recv()
    total = audio_sum[...]
    loss = loss_sum[...]
    for d in range(side - 1):
        total += audio_in[d].astype(F32)
        loss += loss_in[d]
    loss_ref[...] = loss / group
    audio_unit, audio_len = unit_rows(audio_ref[...])
    audio_grad_ref[...] = back_through_norm(audio_unit, audio_len, total)
    for d in range(side - 1):
        text_sum[...] += text_in[d].astype(F32)
    for copy in near + sent + label_steps:
        copy.wait_send()
    pltpu.make_async_copy(out_rows, out_rows, rows_send.at[0]).wait()

    pick_back = jnp.where(iota((row_count, slot_count), 1) == slot_column, 1.0, 0.0).astype(BF16)
    total = text_sum[...]
    for chunk in range(CHUNKS):
        span = slice(chunk * 2 * pairs * CAPACITY, (chunk + 1) * 2 * pairs * CAPACITY)
        wait_blocks(in_reply, reply_recv, chunk)
        read_blocks(in_reply, slots, chunks, pl.ds(chunk * pairs, pairs))
        total += dot_nn(pick_back[:, span], slots[span])
    text_unit, text_len = unit_rows(text_ref[...])
    text_grad_ref[...] = back_through_norm(text_unit, text_len, total)
    pltpu.make_async_copy(out_reply, out_reply, reply_send.at[0]).wait()


def body(audio, text, labels, route, scale, bias):
    row_count, width = audio.shape
    wide_size = lax.axis_size("wide")
    side = math.isqrt(lax.axis_size("narrow"))
    slot_count = wide_size * CAPACITY
    vmem = pl.BlockSpec(memory_space=pltpu.VMEM)
    smem = pl.BlockSpec(memory_space=pltpu.SMEM)
    blocks = pltpu.VMEM((wide_size // 2, 2, CAPACITY * width // LANES, LANES), BF16)
    inner = 8 if wide_size >= 64 else 2
    near_labels = pltpu.VMEM((inner, 1, LANES), F32)
    far_labels = pltpu.VMEM((wide_size // inner, 1, LANES), F32)
    rows = pltpu.VMEM((row_count, width), BF16)
    numbers = pltpu.VMEM((1, row_count), jnp.int32)
    whole = pl.BlockSpec(memory_space=pl.ANY)
    gathered = pltpu.VMEM((side, row_count, width), BF16)
    gathered_labels = pltpu.VMEM((side, 1, row_count), F32)
    term = pltpu.VMEM((row_count, width), F32)
    parts = pltpu.VMEM((side - 1, row_count, width), BF16)
    part_losses = pltpu.VMEM((side - 1, 1, row_count), F32)
    one_sem = pltpu.SemaphoreType.DMA((1,))
    chunk_sem = pltpu.SemaphoreType.DMA((CHUNKS,))
    label_sem = pltpu.SemaphoreType.DMA((2, max(inner, wide_size // inner)))
    near_sem = pltpu.SemaphoreType.DMA((7, side))
    row_loss, audio_grad, text_grad = pl.pallas_call(
        functools.partial(kernel, wide_size, side),
        out_shape=(
            jax.ShapeDtypeStruct((1, row_count), F32),
            jax.ShapeDtypeStruct((row_count, width), F32),
            jax.ShapeDtypeStruct((row_count, width), F32),
        ),
        in_specs=[smem, smem, whole, whole, whole, whole],
        out_specs=(vmem, vmem, vmem),
        scratch_shapes=[
            rows, rows, numbers, numbers,
            blocks, blocks, blocks, blocks, pltpu.VMEM((2, CAPACITY * width // LANES, LANES), BF16),
            pltpu.VMEM((slot_count, width), BF16),
            near_labels, near_labels, far_labels, far_labels,
            gathered, gathered, gathered_labels, gathered_labels,
            pltpu.VMEM((side, side, row_count, row_count), BF16),
            term, term, pltpu.VMEM((1, row_count), F32),
            parts, parts, parts, parts, part_losses, part_losses,
            one_sem, chunk_sem, one_sem, chunk_sem,
            label_sem, label_sem, near_sem, near_sem, pltpu.SemaphoreType.DMA((4,)),
        ],
        compiler_params=pltpu.CompilerParams(
            collective_id=0, has_side_effects=True, vmem_limit_bytes=56 * 2**20
        ),
    )(scale, bias, audio, text, labels.reshape(1, row_count), route.reshape(1, row_count))
    return (row_loss.reshape(row_count), audio_grad, text_grad)


def solution(mesh):
    rows = P(("wide", "narrow"), None)
    return jax.shard_map(
        body,
        mesh=mesh,
        in_specs=(rows, rows, P(("wide", "narrow")), rows, P(), P()),
        out_specs=(P(("wide", "narrow")), rows, rows),
        check_vma=False,
    )
```
